512 devices in a mesh: chan: 16 (over y_hi, z), ctx: 32 (over y_lo, x, core).
Axes of the slice: x: 4, y: 8 (y_hi: 2, y_lo: 4; y = y_hi * 4 + y_lo), z: 8, core: 2. Of those that a mesh axis runs over, the one named last changes fastest.
Arguments:
- features: float32 [3, 4096, 8192], P(None, 'chan', 'ctx'), may hold values from -6 to 6
- short_conv: float32 [3, 4096, 3], P(None, 'chan'), may hold values from -3 to 3
- filters: float32 [4096, 8192], P('chan', 'ctx'), may hold values from -0.0625 to 0.0625
- skip_gain: float32 [4096], P('chan'), may hold values from 0.5 to 1.5
Outputs:
- mixed: float32 [4096, 8192], P('chan', 'ctx')
The draws below stay inside these ranges and needn't reach their ends.
All inputs are finite; a program needn't handle non-finite values.
Results may differ from the reference program's by a relative error of at most 0.000064.
Values sent between devices are 32-bit elements; how exact they have to be, the bound alone decides.
A program may use at most 64 MiB of HBM per device.

```python
import jax
import jax.numpy as jnp
from jax import lax

CHANNELS = 4096
SEQ = 8192


def block_scale(rng, shape, cuts, smallest, largest):
    factor_of, own = 1.0, jax.random.fold_in(rng, 6)
    for position, parts in cuts:
        draws = jnp.exp(jax.random.uniform(jax.random.fold_in(own, position), (parts,), jnp.float32, smallest / len(cuts), largest / len(cuts)))
        factor_of = factor_of * jnp.repeat(draws, shape[position] // parts).reshape([-1 if axis == position else 1 for axis in range(len(shape))])
    return factor_of


def scatter_about(own_key, extent, width, most, cuts=(), kind=jnp.bfloat16):
    array = width * jax.random.normal(own_key, extent, jnp.float32)
    if cuts:
        array = array * block_scale(own_key, extent, cuts, -0.22, 0.18)
    return jnp.clip(array, -most, most).astype(kind)


def setup_inputs(seed: int = 0) -> dict:
    arg_keys = jax.random.split(jax.random.key(seed), 5)
    return {
        "features": scatter_about(arg_keys[0], (3, CHANNELS, SEQ), 1.0, 6.0, ((1, 16), (2, 32)), jnp.float32),
        "short_conv": scatter_about(arg_keys[1], (3, CHANNELS, 3), 0.6, 3.0, ((1, 16),), jnp.float32),
        "filters": scatter_about(arg_keys[2], (CHANNELS, SEQ), SEQ ** -0.5, 0.0625, ((0, 16), (1, 32)), jnp.float32),
        "skip_gain": jnp.clip(0.5 + 1.0 * jax.random.uniform(arg_keys[3], (CHANNELS,), jnp.float32) ** block_scale(arg_keys[3], (CHANNELS,), ((0, 16),), -0.2, 0.2), 0.5, 1.5),
    }


def reference(features, short_conv, filters, skip_gain):
    seq_len = features.shape[2]
    padded = jnp.pad(features, ((0, 0), (0, 0), (2, 0)))
    featured = short_conv[:, :, 0:1] * padded[:, :, 2:] + short_conv[:, :, 1:2] * padded[:, :, 1:-1] + short_conv[:, :, 2:3] * padded[:, :, :-2]
    queries = featured[0]
    gated_kv = featured[1] * featured[2]
    fft_len = 2 * seq_len

    def one_channel(pair):
        signal, kernel = pair
        spectrum = jnp.fft.rfft(signal, n=fft_len) * jnp.fft.rfft(kernel, n=fft_len)
        return jnp.fft.irfft(spectrum, n=fft_len)[:seq_len]

    convolved = lax.map(one_channel, (gated_kv, filters))
    return queries * (convolved + skip_gain[:, None] * gated_kv)
```

```python
import functools

import jax
import jax.numpy as jnp
import numpy as np
from jax import lax
from jax.experimental import pallas as pl
from jax.experimental.pallas import tpu as pltpu
from jax.sharding import PartitionSpec as P

MESH = pl.DeviceIdType.MESH
TILE = 128
PAD = 4
GROUP = 4
LIMIT = 63 * 2**20


def tables(size):
    n, k = np.arange(size)[:, None], np.arange(size)[None, :]
    angle = np.pi * (n * k % (2 * size)) / size
    last = np.where(n % 2 == 0, 1.0, -1.0)
    forward = np.concatenate([np.cos(angle), np.where(k == 0, last, -np.sin(angle))], axis=1)
    weight = np.where(np.arange(size) == 0, 0.5, 1.0) / size
    backward = (forward * np.concatenate([weight, weight])[None, :]).T
    return forward.astype(np.float32), backward.astype(np.float32)


def split(x):
    high = x.astype(jnp.bfloat16)
    return high, (x - high.astype(jnp.float32)).astype(jnp.bfloat16)


def dot3(x, table_high, table_low):
    high, low = split(x)
    dot = functools.partial(jnp.dot, preferred_element_type=jnp.float32)
    return dot(high, table_high[...]) + (dot(low, table_high[...]) + dot(high, table_low[...]))


def kernel(
    n, feat_hbm, taps_hbm, filt_hbm, skip_hbm, forward_hbm, backward_hbm, out_ref,
    feat, filt, taps_ref, skip_ref, forward, backward, fwd_high, fwd_low, bwd_high, bwd_low, rim_out, rim_in, queries, gated, got_f, got_g,
    f_re, f_im, f_sum, g_re, g_im, g_sum, conv_out, conv_in,
    load_sem, rim_send, rim_recv, send_sem, recv_sem,
):
    me = lax.axis_index("ctx")
    channels, tokens = filt.shape
    per = channels // n

    barrier = pltpu.get_barrier_semaphore()

    def greet(step, carry):
        pl.semaphore_signal(barrier, inc=1, device_id={"ctx": lax.rem(me + step, n)}, device_id_type=MESH)
        return carry

    lax.fori_loop(1, n, greet, 0, unroll=True)

    loads = [
        pltpu.make_async_copy(src, dst, load_sem.at[i])
        for i, (src, dst) in enumerate(
            [(feat_hbm, feat), (taps_hbm, taps_ref), (skip_hbm, skip_ref), (filt_hbm, filt), (forward_hbm, forward), (backward_hbm, backward)]
        )
    ]
    for load in loads:
        load.start()

    for load in loads[:3]:
        load.wait()
    scalars = jnp.concatenate(
        [taps_ref[0], taps_ref[1], taps_ref[2], skip_ref[...], jnp.zeros((TILE - 10, channels), jnp.float32)], axis=0
    )
    columns = jnp.transpose(scalars)

    lane = lax.broadcasted_iota(jnp.int32, (channels, TILE), 1)
    ends = [feat[s, :, tokens - TILE :] for s in range(3)]
    merged = jnp.where(
        lane >= TILE - 2,
        ends[2],
        jnp.where(lane >= TILE - 4, pltpu.roll(ends[1], TILE - 2, 1), pltpu.roll(ends[0], TILE - 4, 1)),
    )
    rim_out[...] = jnp.transpose(merged)[TILE - 8 :, :]
    loads[3].wait()

    pl.semaphore_wait(barrier, n - 1)

    rim = pltpu.make_async_remote_copy(
        src_ref=rim_out, dst_ref=rim_in, send_sem=rim_send, recv_sem=rim_recv,
        device_id={"ctx": lax.rem(me + 1, n)}, device_id_type=MESH,
    )
    rim.start()

    def rows(t):
        return pl.ds(pl.multiple_of(t * per, per), per)

    def scatter(source, target, which):
        def send(step, carry):
            t = lax.rem(me + step, n)
            pltpu.make_async_remote_copy(
                src_ref=source.at[rows(t)], dst_ref=target.at[me], send_sem=send_sem.at[which], recv_sem=recv_sem.at[which],
                device_id={"ctx": t}, device_id_type=MESH,
            ).start()
            return carry

        lax.fori_loop(1, n, send, 0, unroll=True)
        pltpu.make_async_copy(source.at[rows(me)], target.at[me], recv_sem.at[which]).start()

    def wait_all(target, which):
        pltpu.make_async_copy(target, target, recv_sem.at[which]).wait()

    scatter(filt, got_f, 0)

    rim.wait()
    rims = jnp.transpose(jnp.concatenate([jnp.zeros((TILE - 8, channels), jnp.float32), rim_in[...]], axis=0))
    rims = jnp.where(me == 0, jnp.zeros_like(rims), rims)

    def featured(s):
        before = [pltpu.roll(rims, 2 * (2 - s) + lag, 1) for lag in (1, 2)]
        taps = [jnp.broadcast_to(columns[:, 3 * s + j : 3 * s + j + 1], (channels, TILE)) for j in range(3)]
        parts = []
        for tile in range(tokens // TILE):
            own = feat[s, :, tile * TILE : (tile + 1) * TILE]
            total = taps[0] * own
            turned = []
            for lag in (1, 2):
                now = pltpu.roll(own, lag, 1)
                total = total + taps[lag] * jnp.where(lane < lag, before[lag - 1], now)
                turned.append(now)
            before = turned
            parts.append(total)
        return parts

    keys, values = featured(1), featured(2)
    for tile in range(tokens // TILE):
        gated[:, tile * TILE : (tile + 1) * TILE] = keys[tile] * values[tile]
    scatter(gated, got_g, 1)
    for tile, part in enumerate(featured(0)):
        queries[:, tile * TILE : (tile + 1) * TILE] = part

    for load in loads[4:]:
        load.wait()
    fwd_high[...], fwd_low[...] = split(forward[...])
    bwd_high[...], bwd_low[...] = split(backward[...])
    wait_all(got_f, 0)
    spectrum = dot3(got_f[...].reshape(channels, tokens), fwd_high, fwd_low)
    real, imag = spectrum[:, :tokens], spectrum[:, tokens:]
    f_re[...] = real.reshape(n, per, tokens)
    f_im[...] = imag.reshape(n, per, tokens)
    f_sum[...] = (real + imag).reshape(n, per, tokens)
    wait_all(got_g, 1)
    spectrum = dot3(got_g[...].reshape(channels, tokens), fwd_high, fwd_low)
    sign = (1 - 2 * (lax.broadcasted_iota(jnp.int32, (1, 1, tokens), 2) % 2)).astype(jnp.float32)
    nothing = jnp.zeros((PAD, per, tokens), jnp.float32)
    sums = []
    for half, store in ((0, g_re), (1, g_im)):
        bins = spectrum[:, half * tokens : (half + 1) * tokens].reshape(n, per, tokens)
        late = jnp.concatenate([nothing[:1], bins[:-1]], axis=0)
        total = bins + sign * late
        store[:PAD] = nothing
        store[PAD:] = total
        sums.append(total)
    g_sum[:PAD] = nothing
    g_sum[PAD:] = sums[0] + sums[1]

    row = 8
    first_lane = lax.broadcasted_iota(jnp.int32, (1, 1, TILE), 2) == 0
    for start in range(0, n, row):
        pieces = {}
        for tile in range(tokens // TILE):
            at = slice(tile * TILE, (tile + 1) * TILE)
            for base in range(start, start + row, GROUP):

                def step(m, acc, base=base, at=at):
                    acc = list(acc)
                    fs = [[ref[GROUP * m + b, :, at] for ref in (f_re, f_im, f_sum)] for b in range(GROUP)]
                    g0 = base - GROUP * m + PAD
                    gs = {d: [ref[g0 + d, :, at] for ref in (g_re, g_im, g_sum)] for d in range(1 - GROUP, GROUP)}
                    for a in range(GROUP):
                        for b in range(GROUP):
                            for part in range(3):
                                acc[3 * a + part] = acc[3 * a + part] + fs[b][part] * gs[a - b][part]
                    return tuple(acc)

                zero = jnp.zeros((per, TILE), jnp.float32)
                acc = lax.fori_loop(0, base // GROUP + 1, step, (zero,) * (3 * GROUP))
                for a in range(GROUP):
                    pieces[tile, base - start + a] = acc[3 * a : 3 * a + 3]
        real_parts, imag_parts = [], []
        for tile in range(tokens // TILE):
            both, cross, mixed_sum = (jnp.concatenate([pieces[tile, a][part] for a in range(row)], axis=0) for part in range(3))
            re, im = both - cross, mixed_sum - both - cross
            if tile == 0:
                packed = lax.broadcasted_iota(jnp.int32, (row * per, TILE), 1) == 0
                re, im = jnp.where(packed, both, re), jnp.where(packed, cross, im)
            real_parts.append(re)
            imag_parts.append(im)
        back = dot3(jnp.concatenate(real_parts + imag_parts, axis=1), bwd_high, bwd_low)
        conv_out[start : start + row] = back.reshape(row, per, tokens)
        for block in range(start, start + row):

            @pl.when(me != block)
            def _(block=block):
                pltpu.make_async_remote_copy(
                    src_ref=conv_out.at[block], dst_ref=conv_in.at[me], send_sem=send_sem.at[2], recv_sem=recv_sem.at[2],
                    device_id={"ctx": block}, device_id_type=MESH,
                ).start()

            @pl.when(me == block)
            def _(block=block):
                pltpu.make_async_copy(conv_out.at[block], conv_in.at[me], recv_sem.at[2]).start()

    wait_all(conv_in, 2)
    skip = jnp.broadcast_to(columns[:, 9:10], (channels, TILE))
    convolved = conv_in[...].reshape(channels, tokens)
    for tile in range(tokens // TILE):
        at = slice(tile * TILE, (tile + 1) * TILE)
        out_ref[:, at] = queries[:, at] * (convolved[:, at] + skip * gated[:, at])
    for which in range(3):
        sent = got_f.at[pl.ds(0, n - 1)]
        pltpu.make_async_copy(sent, sent, send_sem.at[which]).wait()


def solution(mesh):
    n = mesh.shape["ctx"]

    def shards(features, short_conv, filters, skip_gain):
        channels, tokens = filters.shape
        per = channels // n
        any_space, vmem = pl.BlockSpec(memory_space=pl.ANY), pl.BlockSpec(memory_space=pltpu.VMEM)
        real = functools.partial(pltpu.VMEM, dtype=jnp.float32)
        block = (n, per, tokens)
        padded = (n + PAD, per, tokens)
        return pl.pallas_call(
            functools.partial(kernel, n),
            out_shape=jax.ShapeDtypeStruct((channels, tokens), jnp.float32),
            in_specs=[any_space] * 6,
            out_specs=vmem,
            scratch_shapes=[
                real((3, channels, tokens)),
                real((channels, tokens)),
                real((3, 3, channels)),
                real((1, channels)),
                real((tokens, 2 * tokens)),
                real((2 * tokens, tokens)),
                pltpu.VMEM((tokens, 2 * tokens), jnp.bfloat16),
                pltpu.VMEM((tokens, 2 * tokens), jnp.bfloat16),
                pltpu.VMEM((2 * tokens, tokens), jnp.bfloat16),
                pltpu.VMEM((2 * tokens, tokens), jnp.bfloat16),
                real((8, channels)),
                real((8, channels)),
                real((channels, tokens)),
                real((channels, tokens)),
                real(block),
                real(block),
                real(block),
                real(block),
                real(block),
                real(padded),
                real(padded),
                real(padded),
                real(block),
                real(block),
                pltpu.SemaphoreType.DMA((6,)),
                pltpu.SemaphoreType.DMA,
                pltpu.SemaphoreType.DMA,
                pltpu.SemaphoreType.DMA((3,)),
                pltpu.SemaphoreType.DMA((3,)),
            ],
            compiler_params=pltpu.CompilerParams(collective_id=0, has_side_effects=True, vmem_limit_bytes=LIMIT),
        )(features, jnp.transpose(short_conv, (0, 2, 1)), filters, skip_gain.reshape(1, channels), *(jnp.asarray(t) for t in tables(tokens)))

    placed = (P(None, "chan", "ctx"), P(None, "chan", None), P("chan", "ctx"), P("chan"))
    return jax.shard_map(shards, mesh=mesh, in_specs=placed, out_specs=P("chan", "ctx"), check_vma=False)
```

```python
import functools

import jax
import jax.numpy as jnp
import numpy as np
from jax import lax
from jax.experimental import pallas as pl
from jax.experimental.pallas import tpu as pltpu
from jax.sharding import PartitionSpec as P

MESH = pl.DeviceIdType.MESH
TILE = 128
PAD = 4
GROUP = 4
LIMIT = 63 * 2**20


def tables(size):
    n, k = np.arange(size)[:, None], np.arange(size)[None, :]
    angle = np.pi * (n * k % (2 * size)) / size
    last = np.where(n % 2 == 0, 1.0, -1.0)
    forward = np.concatenate([np.cos(angle), np.where(k == 0, last, -np.sin(angle))], axis=1)
    weight = np.where(np.arange(size) == 0, 0.5, 1.0) / size
    backward = (forward * np.concatenate([weight, weight])[None, :]).T
    return forward.astype(np.float32), backward.astype(np.float32)


def split(x):
    high = x.astype(jnp.bfloat16)
    return high, (x - high.astype(jnp.float32)).astype(jnp.bfloat16)


def dot3(x, table_high, table_low):
    high, low = split(x)
    dot = functools.partial(jnp.dot, preferred_element_type=jnp.float32)
    return dot(high, table_high[...]) + (dot(low, table_high[...]) + dot(high, table_low[...]))


def swap(first, second):
    half = first.shape[1] // 2
    low = lax.broadcasted_iota(jnp.int32, first.shape, 1) < half
    return jnp.where(low, first, pltpu.roll(second, half, 1)), jnp.where(low, pltpu.roll(first, half, 1), second)


def pairs(blocks):
    split_up = blocks.reshape(blocks.shape[0] // 2, 2, *blocks.shape[1:])
    return swap(split_up[:, 0], split_up[:, 1])


def unpairs(tile0, tile1):
    joined = jnp.stack(swap(tile0, tile1), axis=1)
    return joined.reshape(2 * tile0.shape[0], *tile0.shape[1:])


def kernel(
    n, feat_hbm, taps_hbm, filt_hbm, skip_hbm, forward_hbm, backward_hbm, out_ref,
    feat, filt, taps_ref, skip_ref, forward, backward, fwd_high, fwd_low, bwd_high, bwd_low, rim_out, rim_in, queries, gated, sent_f, sent_g,
    got_f, got_g, f_re, f_im, f_sum, g_re, g_im, g_sum, conv_out, conv_in,
    load_sem, rim_send, rim_recv, send_sem, recv_sem,
):
    me = lax.axis_index("ctx")
    channels, tokens = filt.shape
    per = channels // n
    chunks = 2

    barrier = pltpu.get_barrier_semaphore()

    def greet(step, carry):
        pl.semaphore_signal(barrier, inc=1, device_id={"ctx": lax.rem(me + step, n)}, device_id_type=MESH)
        return carry

    lax.fori_loop(1, n, greet, 0, unroll=True)

    loads = [
        pltpu.make_async_copy(src, dst, load_sem.at[i])
        for i, (src, dst) in enumerate(
            [(feat_hbm, feat), (taps_hbm, taps_ref), (skip_hbm, skip_ref), (filt_hbm, filt), (forward_hbm, forward), (backward_hbm, backward)]
        )
    ]
    for load in loads:
        load.start()
    for load in loads[:3]:
        load.wait()
    scalars = jnp.concatenate(
        [taps_ref[0], taps_ref[1], taps_ref[2], skip_ref[...], jnp.zeros((TILE - 10, channels), jnp.float32)], axis=0
    )
    columns = jnp.transpose(scalars)

    def column(i):
        return jnp.broadcast_to(columns[:, i : i + 1], (channels, TILE))

    lane = lax.broadcasted_iota(jnp.int32, (channels, TILE), 1)
    ends = [feat[s, :, tokens - TILE :] for s in range(3)]
    merged = jnp.where(
        lane >= TILE - 2,
        ends[2],
        jnp.where(lane >= TILE - 4, pltpu.roll(ends[1], TILE - 2, 1), pltpu.roll(ends[0], TILE - 4, 1)),
    )
    rim_out[...] = jnp.transpose(merged)[TILE - 8 :, :]

    def pack(tile0, tile1, target):
        target[0], target[1] = swap(tile0.reshape(n, per, TILE), tile1.reshape(n, per, TILE))

    loads[3].wait()
    pack(filt[:, :TILE], filt[:, TILE:], sent_f)

    pl.semaphore_wait(barrier, n - 1)

    rim = pltpu.make_async_remote_copy(
        src_ref=rim_out, dst_ref=rim_in, send_sem=rim_send, recv_sem=rim_recv,
        device_id={"ctx": lax.rem(me + 1, n)}, device_id_type=MESH,
    )
    rim.start()

    def scatter(source, target, which, chunk):
        def send(step, carry):
            t = lax.rem(me + step, n)
            pltpu.make_async_remote_copy(
                src_ref=source.at[chunk, t], dst_ref=target.at[chunk, me], send_sem=send_sem.at[which, chunk], recv_sem=recv_sem.at[which, chunk],
                device_id={"ctx": t}, device_id_type=MESH,
            ).start()
            return carry

        lax.fori_loop(1, n, send, 0, unroll=True)
        pltpu.make_async_copy(source.at[chunk, me], target.at[chunk, me], recv_sem.at[which, chunk]).start()

    def wait_all(target, which, chunk):
        pltpu.make_async_copy(target.at[chunk], target.at[chunk], recv_sem.at[which, chunk]).wait()

    scatter(sent_f, got_f, 0, 0)
    for load in loads[4:]:
        load.wait()
    fwd_high[...], fwd_low[...] = split(forward[...])
    bwd_high[...], bwd_low[...] = split(backward[...])

    rim.wait()
    rims = jnp.transpose(jnp.concatenate([jnp.zeros((TILE - 8, channels), jnp.float32), rim_in[...]], axis=0))
    rims = jnp.where(me == 0, jnp.zeros_like(rims), rims)

    def featured(s):
        before = [pltpu.roll(rims, 2 * (2 - s) + lag, 1) for lag in (1, 2)]
        taps = [column(3 * s + j) for j in range(3)]
        parts = []
        for tile in range(tokens // TILE):
            own = feat[s, :, tile * TILE : (tile + 1) * TILE]
            total = taps[0] * own
            turned = []
            for lag in (1, 2):
                now = pltpu.roll(own, lag, 1)
                total = total + taps[lag] * jnp.where(lane < lag, before[lag - 1], now)
                turned.append(now)
            before = turned
            parts.append(total)
        return parts

    keys, values = featured(1), featured(2)
    products = [k * v for k, v in zip(keys, values)]
    pack(*products, sent_g)
    scatter(sent_g, got_g, 1, 0)
    scatter(sent_f, got_f, 0, 1)
    scatter(sent_g, got_g, 1, 1)
    skip = column(9)
    for tile, part in enumerate(featured(0)):
        at = slice(tile * TILE, (tile + 1) * TILE)
        queries[:, at] = part
        gated[:, at] = skip * products[tile]

    def spectrum(blocks):
        rows = jnp.concatenate(pairs(blocks), axis=2).reshape(n * per // 2, tokens)
        bins = dot3(rows, fwd_high, fwd_low)
        tiles = [bins[:, i * TILE : (i + 1) * TILE].reshape(n // 2, per, TILE) for i in range(4)]
        return unpairs(tiles[0], tiles[1]), unpairs(tiles[2], tiles[3])

    sign = (1 - 2 * (lax.broadcasted_iota(jnp.int32, (1, 1, TILE), 2) % 2)).astype(jnp.float32)
    nothing = jnp.zeros((PAD, per, TILE), jnp.float32)
    stage_blocks = n // 2

    def filter_spectra(chunk):
        wait_all(got_f, 0, chunk)
        real, imag = spectrum(got_f[chunk])
        f_re[...], f_im[...], f_sum[...] = real, imag, real + imag

    def signal_spectra(chunk):
        wait_all(got_g, 1, chunk)
        sums = []
        for part, store in zip(spectrum(got_g[chunk]), (g_re, g_im)):
            late = jnp.concatenate([nothing[:1], part[:-1]], axis=0)
            total = part + sign * late
            store[:PAD] = nothing
            store[PAD:] = total
            sums.append(total)
        g_sum[:PAD] = nothing
        g_sum[PAD:] = sums[0] + sums[1]

    def convolve(chunk):
        for stage in range(2):
            start = stage_blocks * lax.rem(me // stage_blocks + 1 + stage, 2)
            pieces = []
            for first in range(0, stage_blocks, GROUP):
                base = start + first

                def step(m, acc, base=base):
                    acc = list(acc)
                    fs = [[ref[GROUP * m + b] for ref in (f_re, f_im, f_sum)] for b in range(GROUP)]
                    g0 = base - GROUP * m + PAD
                    gs = {d: [ref[g0 + d] for ref in (g_re, g_im, g_sum)] for d in range(1 - GROUP, GROUP)}
                    for a in range(GROUP):
                        for b in range(GROUP):
                            for part in range(3):
                                acc[3 * a + part] = acc[3 * a + part] + fs[b][part] * gs[a - b][part]
                    return tuple(acc)

                zero = jnp.zeros((per, TILE), jnp.float32)
                acc = lax.fori_loop(0, base // GROUP + 1, step, (zero,) * (3 * GROUP))
                pieces += [acc[3 * a : 3 * a + 3] for a in range(GROUP)]
            both, cross, total = (jnp.stack([piece[part] for piece in pieces], axis=0) for part in range(3))
            real, imag = both - cross, total - both - cross
            packed = (lax.broadcasted_iota(jnp.int32, real.shape, 2) == 0) & (lax.broadcasted_iota(jnp.int32, real.shape, 1) < per // 2)
            real, imag = jnp.where(packed, both, real), jnp.where(packed, cross, imag)
            rows = jnp.concatenate([*pairs(real), *pairs(imag)], axis=2).reshape(stage_blocks * per // 2, 2 * tokens)
            back = dot3(rows, bwd_high, bwd_low)
            tiles = [back[:, i * TILE : (i + 1) * TILE].reshape(stage_blocks // 2, per, TILE) for i in range(2)]
            conv_out[chunk, pl.ds(start, stage_blocks)] = unpairs(*tiles)

            def send(i, carry, start=start):
                t = start + lax.rem(me + i, stage_blocks)
                pltpu.make_async_remote_copy(
                    src_ref=conv_out.at[chunk, t], dst_ref=conv_in.at[chunk, me], send_sem=send_sem.at[2, chunk], recv_sem=recv_sem.at[2, chunk],
                    device_id={"ctx": t}, device_id_type=MESH,
                ).start()
                return carry

            lax.fori_loop(stage, stage_blocks, send, 0, unroll=True)
        pltpu.make_async_copy(conv_out.at[chunk, me], conv_in.at[chunk, me], recv_sem.at[2, chunk]).start()

    for chunk in range(chunks):
        filter_spectra(chunk)
        signal_spectra(chunk)
        convolve(chunk)

    for chunk in range(chunks):
        wait_all(conv_in, 2, chunk)
    for tile, part in enumerate(swap(conv_in[0], conv_in[1])):
        at = slice(tile * TILE, (tile + 1) * TILE)
        out_ref[:, at] = queries[:, at] * (part.reshape(channels, TILE) + gated[:, at])
    for which in range(3):
        for chunk in range(chunks):
            sent = got_f.at[chunk, pl.ds(0, n - 1)]
            pltpu.make_async_copy(sent, sent, send_sem.at[which, chunk]).wait()


def solution(mesh):
    n = mesh.shape["ctx"]

    def shards(features, short_conv, filters, skip_gain):
        channels, tokens = filters.shape
        per = channels // n
        any_space, vmem = pl.BlockSpec(memory_space=pl.ANY), pl.BlockSpec(memory_space=pltpu.VMEM)
        real = functools.partial(pltpu.VMEM, dtype=jnp.float32)
        moved, spectra, padded = (2, n, per, TILE), (n, per, TILE), (n + PAD, per, TILE)
        return pl.pallas_call(
            functools.partial(kernel, n),
            out_shape=jax.ShapeDtypeStruct((channels, tokens), jnp.float32),
            in_specs=[any_space] * 6,
            out_specs=vmem,
            scratch_shapes=[
                real((3, channels, tokens)),
                real((channels, tokens)),
                real((3, 3, channels)),
                real((1, channels)),
                real((tokens, 2 * tokens)),
                real((2 * tokens, tokens)),
                pltpu.VMEM((tokens, 2 * tokens), jnp.bfloat16),
                pltpu.VMEM((tokens, 2 * tokens), jnp.bfloat16),
                pltpu.VMEM((2 * tokens, tokens), jnp.bfloat16),
                pltpu.VMEM((2 * tokens, tokens), jnp.bfloat16),
                real((8, channels)),
                real((8, channels)),
                real((channels, tokens)),
                real((channels, tokens)),
                real(moved),
                real(moved),
                real(moved),
                real(moved),
                real(spectra),
                real(spectra),
                real(spectra),
                real(padded),
                real(padded),
                real(padded),
                real(moved),
                real(moved),
                pltpu.SemaphoreType.DMA((6,)),
                pltpu.SemaphoreType.DMA,
                pltpu.SemaphoreType.DMA,
                pltpu.SemaphoreType.DMA((3, 2)),
                pltpu.SemaphoreType.DMA((3, 2)),
            ],
            compiler_params=pltpu.CompilerParams(collective_id=0, has_side_effects=True, vmem_limit_bytes=LIMIT),
        )(features, jnp.transpose(short_conv, (0, 2, 1)), filters, skip_gain.reshape(1, channels), *(jnp.asarray(t) for t in tables(tokens)))

    placed = (P(None, "chan", "ctx"), P(None, "chan", None), P("chan", "ctx"), P("chan"))
    return jax.shard_map(shards, mesh=mesh, in_specs=placed, out_specs=P("chan", "ctx"), check_vma=False)
```

```python
import functools

import jax
import jax.numpy as jnp
import numpy as np
from jax import lax
from jax.experimental import pallas as pl
from jax.experimental.pallas import tpu as pltpu
from jax.sharding import PartitionSpec as P

MESH = pl.DeviceIdType.MESH
TILE = 128
PAD = 4
GROUP = 4
LIMIT = 63 * 2**20


def tables(size):
    n, k = np.arange(size)[:, None], np.arange(size)[None, :]
    angle = np.pi * (n * k % (2 * size)) / size
    last = np.where(n % 2 == 0, 1.0, -1.0)
    forward = np.concatenate([np.cos(angle), np.where(k == 0, last, -np.sin(angle))], axis=1)
    weight = np.where(np.arange(size) == 0, 0.5, 1.0) / size
    backward = (forward * np.concatenate([weight, weight])[None, :]).T
    return forward.astype(np.float32), backward.astype(np.float32)


def split(x):
    high = x.astype(jnp.bfloat16)
    return high, (x - high.astype(jnp.float32)).astype(jnp.bfloat16)


def dot3(x, table_high, table_low):
    high, low = split(x)
    dot = functools.partial(jnp.dot, preferred_element_type=jnp.float32)
    return dot(high, table_high[...]) + (dot(low, table_high[...]) + dot(high, table_low[...]))


def swap(first, second):
    half = first.shape[1] // 2
    low = lax.broadcasted_iota(jnp.int32, first.shape, 1) < half
    return jnp.where(low, first, pltpu.roll(second, half, 1)), jnp.where(low, pltpu.roll(first, half, 1), second)


def pairs(blocks):
    split_up = blocks.reshape(blocks.shape[0] // 2, 2, *blocks.shape[1:])
    return swap(split_up[:, 0], split_up[:, 1])


def unpairs(tile0, tile1):
    joined = jnp.stack(swap(tile0, tile1), axis=1)
    return joined.reshape(2 * tile0.shape[0], *tile0.shape[1:])


def kernel(
    n, feat_hbm, taps_hbm, filt_hbm, skip_hbm, forward_hbm, backward_hbm, conv_in, queries_out, gated_out,
    feat, filt, taps_ref, skip_ref, forward, backward, fwd_high, fwd_low, bwd_high, bwd_low, rim_out, rim_in, queries, gated, sent_f, sent_g,
    got_f, got_g, f_re, f_im, f_sum, g_re, g_im, g_sum, conv_out,
    load_sem, store_sem, rim_send, rim_recv, send_sem, recv_sem,
):
    me = lax.axis_index("ctx")
    channels, tokens = filt.shape
    per = channels // n
    chunks = 2

    barrier = pltpu.get_barrier_semaphore()

    def greet(step, carry):
        pl.semaphore_signal(barrier, inc=1, device_id={"ctx": lax.rem(me + step, n)}, device_id_type=MESH)
        return carry

    lax.fori_loop(1, n, greet, 0, unroll=True)

    loads = [
        pltpu.make_async_copy(src, dst, load_sem.at[i])
        for i, (src, dst) in enumerate(
            [(feat_hbm, feat), (taps_hbm, taps_ref), (skip_hbm, skip_ref), (filt_hbm, filt), (forward_hbm, forward), (backward_hbm, backward)]
        )
    ]
    for load in loads:
        load.start()
    for load in loads[:3]:
        load.wait()
    scalars = jnp.concatenate(
        [taps_ref[0], taps_ref[1], taps_ref[2], skip_ref[...], jnp.zeros((TILE - 10, channels), jnp.float32)], axis=0
    )
    columns = jnp.transpose(scalars)

    def column(i):
        return jnp.broadcast_to(columns[:, i : i + 1], (channels, TILE))

    lane = lax.broadcasted_iota(jnp.int32, (channels, TILE), 1)
    ends = [feat[s, :, tokens - TILE :] for s in range(3)]
    merged = jnp.where(
        lane >= TILE - 2,
        ends[2],
        jnp.where(lane >= TILE - 4, pltpu.roll(ends[1], TILE - 2, 1), pltpu.roll(ends[0], TILE - 4, 1)),
    )
    rim_out[...] = jnp.transpose(merged)[TILE - 8 :, :]

    def pack(tile0, tile1, target):
        target[0], target[1] = swap(tile0.reshape(n, per, TILE), tile1.reshape(n, per, TILE))

    loads[3].wait()
    pack(filt[:, :TILE], filt[:, TILE:], sent_f)

    pl.semaphore_wait(barrier, n - 1)

    rim = pltpu.make_async_remote_copy(
        src_ref=rim_out, dst_ref=rim_in, send_sem=rim_send, recv_sem=rim_recv,
        device_id={"ctx": lax.rem(me + 1, n)}, device_id_type=MESH,
    )
    rim.start()

    def scatter(source, target, which, chunk):
        def send(step, carry):
            t = lax.rem(me + step, n)
            pltpu.make_async_remote_copy(
                src_ref=source.at[chunk, t], dst_ref=target.at[chunk, me], send_sem=send_sem.at[which, chunk], recv_sem=recv_sem.at[which, chunk],
                device_id={"ctx": t}, device_id_type=MESH,
            ).start()
            return carry

        lax.fori_loop(1, n, send, 0, unroll=True)
        pltpu.make_async_copy(source.at[chunk, me], target.at[chunk, me], recv_sem.at[which, chunk]).start()

    def wait_all(target, which, chunk):
        pltpu.make_async_copy(target.at[chunk], target.at[chunk], recv_sem.at[which, chunk]).wait()

    scatter(sent_f, got_f, 0, 0)
    for load in loads[4:]:
        load.wait()
    fwd_high[...], fwd_low[...] = split(forward[...])
    bwd_high[...], bwd_low[...] = split(backward[...])

    rim.wait()
    rims = jnp.transpose(jnp.concatenate([jnp.zeros((TILE - 8, channels), jnp.float32), rim_in[...]], axis=0))
    rims = jnp.where(me == 0, jnp.zeros_like(rims), rims)

    def featured(s):
        before = [pltpu.roll(rims, 2 * (2 - s) + lag, 1) for lag in (1, 2)]
        taps = [column(3 * s + j) for j in range(3)]
        parts = []
        for tile in range(tokens // TILE):
            own = feat[s, :, tile * TILE : (tile + 1) * TILE]
            total = taps[0] * own
            turned = []
            for lag in (1, 2):
                now = pltpu.roll(own, lag, 1)
                total = total + taps[lag] * jnp.where(lane < lag, before[lag - 1], now)
                turned.append(now)
            before = turned
            parts.append(total)
        return parts

    keys, values = featured(1), featured(2)
    products = [k * v for k, v in zip(keys, values)]
    pack(*products, sent_g)
    scatter(sent_g, got_g, 1, 0)
    scatter(sent_f, got_f, 0, 1)
    scatter(sent_g, got_g, 1, 1)
    skip = column(9)
    for tile, part in enumerate(featured(0)):
        at = slice(tile * TILE, (tile + 1) * TILE)
        queries[:, at] = part
        gated[:, at] = skip * products[tile]
    stores = [
        pltpu.make_async_copy(src, dst, store_sem.at[i]) for i, (src, dst) in enumerate([(queries, queries_out), (gated, gated_out)])
    ]
    for store in stores:
        store.start()

    def spectrum(blocks):
        rows = jnp.concatenate(pairs(blocks), axis=2).reshape(n * per // 2, tokens)
        bins = dot3(rows, fwd_high, fwd_low)
        tiles = [bins[:, i * TILE : (i + 1) * TILE].reshape(n // 2, per, TILE) for i in range(4)]
        return unpairs(tiles[0], tiles[1]), unpairs(tiles[2], tiles[3])

    turned = lax.axis_index("chan") // (lax.axis_size("chan") // 2)

    def turn(i, blocks):
        row = blocks // 2
        return row * (turned + (1 - 2 * turned) * (i // row)) + lax.rem(i, row)

    sign = (1 - 2 * (lax.broadcasted_iota(jnp.int32, (1, 1, TILE), 2) % 2)).astype(jnp.float32)
    nothing = jnp.zeros((PAD, per, TILE), jnp.float32)
    stage_blocks = n // 2

    def filter_spectra(chunk):
        wait_all(got_f, 0, chunk)
        real, imag = spectrum(got_f[chunk])
        f_re[...], f_im[...], f_sum[...] = real, imag, real + imag

    def signal_spectra(chunk):
        wait_all(got_g, 1, chunk)
        sums = []
        for part, store in zip(spectrum(got_g[chunk]), (g_re, g_im)):
            late = jnp.concatenate([nothing[:1], part[:-1]], axis=0)
            total = part + sign * late
            store[:PAD] = nothing
            store[PAD:] = total
            sums.append(total)
        g_sum[:PAD] = nothing
        g_sum[PAD:] = sums[0] + sums[1]

    def convolve(chunk):
        for stage in range(2):
            start = stage_blocks * lax.rem(me // stage_blocks + 1 + stage, 2)
            pieces = []
            for first in range(0, stage_blocks, GROUP):
                base = start + first

                def step(m, acc, base=base):
                    acc = list(acc)
                    fs = [[ref[GROUP * m + b] for ref in (f_re, f_im, f_sum)] for b in range(GROUP)]
                    g0 = base - GROUP * m + PAD
                    gs = {d: [ref[g0 + d] for ref in (g_re, g_im, g_sum)] for d in range(1 - GROUP, GROUP)}
                    for a in range(GROUP):
                        for b in range(GROUP):
                            for part in range(3):
                                acc[3 * a + part] = acc[3 * a + part] + fs[b][part] * gs[a - b][part]
                    return tuple(acc)

                zero = jnp.zeros((per, TILE), jnp.float32)
                acc = lax.fori_loop(0, base // GROUP + 1, step, (zero,) * (3 * GROUP))
                pieces += [acc[3 * a : 3 * a + 3] for a in range(GROUP)]
            both, cross, total = (jnp.stack([piece[part] for piece in pieces], axis=0) for part in range(3))
            real, imag = both - cross, total - both - cross
            packed = (lax.broadcasted_iota(jnp.int32, real.shape, 2) == 0) & (lax.broadcasted_iota(jnp.int32, real.shape, 1) < per // 2)
            real, imag = jnp.where(packed, both, real), jnp.where(packed, cross, imag)
            rows = jnp.concatenate([*pairs(real), *pairs(imag)], axis=2).reshape(stage_blocks * per // 2, 2 * tokens)
            back = dot3(rows, bwd_high, bwd_low)
            tiles = [back[:, i * TILE : (i + 1) * TILE].reshape(stage_blocks // 2, per, TILE) for i in range(2)]
            conv_out[chunk, pl.ds(start, stage_blocks)] = unpairs(*tiles)

            def send(i, carry, start=start):
                t = start + (turn(i, stage_blocks) if chunk == chunks - 1 else lax.rem(me + i, stage_blocks))
                @pl.when(t != me)
                def _():
                    pltpu.make_async_remote_copy(
                        src_ref=conv_out.at[chunk, t], dst_ref=conv_in.at[chunk, me], send_sem=send_sem.at[2, chunk], recv_sem=recv_sem.at[2, chunk],
                        device_id={"ctx": t}, device_id_type=MESH,
                    ).start()

                return carry

            lax.fori_loop(0, stage_blocks, send, 0, unroll=True)
        pltpu.make_async_copy(conv_out.at[chunk, me], conv_in.at[chunk, me], recv_sem.at[2, chunk]).start()

    for chunk in range(chunks):
        filter_spectra(chunk)
        signal_spectra(chunk)
        convolve(chunk)

    for chunk in range(chunks):
        wait_all(conv_in, 2, chunk)
    for which in range(3):
        for chunk in range(chunks):
            sent = got_f.at[chunk, pl.ds(0, n - 1)]
            pltpu.make_async_copy(sent, sent, send_sem.at[which, chunk]).wait()
    for store in stores:
        store.wait()


def finish(conv_hbm, queries_hbm, gated_hbm, out_hbm, conv, queries, gated, out, load_sem, store_sem):
    parts = load_sem.shape[1]
    n, per = conv.shape[1:3]
    loads, stores = [], []
    for i in range(parts):
        blocks, rows = pl.ds(i * n // parts, n // parts), pl.ds(i * n * per // parts, n * per // parts)
        views = [(conv_hbm.at[:, blocks], conv.at[:, blocks]), (queries_hbm.at[rows], queries.at[rows]), (gated_hbm.at[rows], gated.at[rows])]
        loads.append([pltpu.make_async_copy(src, dst, load_sem.at[j, i]) for j, (src, dst) in enumerate(views)])
        stores.append(pltpu.make_async_copy(out.at[rows], out_hbm.at[rows], store_sem.at[i]))
        for load in loads[-1]:
            load.start()
    for i in range(parts):
        blocks, rows = pl.ds(i * n // parts, n // parts), pl.ds(i * n * per // parts, n * per // parts)
        for load in loads[i]:
            load.wait()
        for tile, part in enumerate(swap(conv[0, blocks], conv[1, blocks])):
            at = slice(tile * TILE, (tile + 1) * TILE)
            out[rows, at] = queries[rows, at] * (part.reshape(n * per // parts, TILE) + gated[rows, at])
        stores[i].start()
    for store in stores:
        store.wait()


def solution(mesh):
    n = mesh.shape["ctx"]

    def shards(features, short_conv, filters, skip_gain):
        channels, tokens = filters.shape
        per = channels // n
        any_space = pl.BlockSpec(memory_space=pl.ANY)
        real = functools.partial(pltpu.VMEM, dtype=jnp.float32)
        moved, spectra, padded = (2, n, per, TILE), (n, per, TILE), (n + PAD, per, TILE)
        whole = jax.ShapeDtypeStruct((channels, tokens), jnp.float32)
        arrived = pl.pallas_call(
            functools.partial(kernel, n),
            out_shape=(jax.ShapeDtypeStruct(moved, jnp.float32), whole, whole),
            in_specs=[any_space] * 6,
            out_specs=(any_space,) * 3,
            scratch_shapes=[
                real((3, channels, tokens)),
                real((channels, tokens)),
                real((3, 3, channels)),
                real((1, channels)),
                real((tokens, 2 * tokens)),
                real((2 * tokens, tokens)),
                pltpu.VMEM((tokens, 2 * tokens), jnp.bfloat16),
                pltpu.VMEM((tokens, 2 * tokens), jnp.bfloat16),
                pltpu.VMEM((2 * tokens, tokens), jnp.bfloat16),
                pltpu.VMEM((2 * tokens, tokens), jnp.bfloat16),
                real((8, channels)),
                real((8, channels)),
                real((channels, tokens)),
                real((channels, tokens)),
                real(moved),
                real(moved),
                real(moved),
                real(moved),
                real(spectra),
                real(spectra),
                real(spectra),
                real(padded),
                real(padded),
                real(padded),
                real(moved),
                pltpu.SemaphoreType.DMA((6,)),
                pltpu.SemaphoreType.DMA((2,)),
                pltpu.SemaphoreType.DMA,
                pltpu.SemaphoreType.DMA,
                pltpu.SemaphoreType.DMA((3, 2)),
                pltpu.SemaphoreType.DMA((3, 2)),
            ],
            compiler_params=pltpu.CompilerParams(collective_id=0, has_side_effects=True, vmem_limit_bytes=LIMIT),
        )(features, jnp.transpose(short_conv, (0, 2, 1)), filters, skip_gain.reshape(1, channels), *(jnp.asarray(t) for t in tables(tokens)))
        parts = 1
        return pl.pallas_call(
            finish,
            out_shape=whole,
            in_specs=[any_space] * 3,
            out_specs=any_space,
            scratch_shapes=[
                real(moved),
                real((channels, tokens)),
                real((channels, tokens)),
                real((channels, tokens)),
                pltpu.SemaphoreType.DMA((3, parts)),
                pltpu.SemaphoreType.DMA((parts,)),
            ],
            compiler_params=pltpu.CompilerParams(vmem_limit_bytes=LIMIT),
        )(*arrived)

    placed = (P(None, "chan", "ctx"), P(None, "chan", None), P("chan", "ctx"), P("chan"))
    return jax.shard_map(shards, mesh=mesh, in_specs=placed, out_specs=P("chan", "ctx"), check_vma=False)
```

```python
import functools

import jax
import jax.numpy as jnp
import numpy as np
from jax import lax
from jax.experimental import pallas as pl
from jax.experimental.pallas import tpu as pltpu
from jax.sharding import PartitionSpec as P

MESH = pl.DeviceIdType.MESH
TILE = 128
PAD = 4
GROUP = 4
LIMIT = 63 * 2**20


def tables(size):
    n, k = np.arange(size)[:, None], np.arange(size)[None, :]
    angle = np.pi * (n * k % (2 * size)) / size
    last = np.where(n % 2 == 0, 1.0, -1.0)
    forward = np.concatenate([np.cos(angle), np.where(k == 0, last, -np.sin(angle))], axis=1)
    weight = np.where(np.arange(size) == 0, 0.5, 1.0) / size
    backward = (forward * np.concatenate([weight, weight])[None, :]).T
    return forward.astype(np.float32), backward.astype(np.float32)


def split(x):
    high = x.astype(jnp.bfloat16)
    return high, (x - high.astype(jnp.float32)).astype(jnp.bfloat16)


def dot3(x, table_high, table_low):
    high, low = split(x)
    dot = functools.partial(jnp.dot, preferred_element_type=jnp.float32)
    return dot(high, table_high[...]) + (dot(low, table_high[...]) + dot(high, table_low[...]))


def swap(first, second):
    half = first.shape[1] // 2
    low = lax.broadcasted_iota(jnp.int32, first.shape, 1) < half
    return jnp.where(low, first, pltpu.roll(second, half, 1)), jnp.where(low, pltpu.roll(first, half, 1), second)


def pairs(blocks):
    split_up = blocks.reshape(blocks.shape[0] // 2, 2, *blocks.shape[1:])
    return swap(split_up[:, 0], split_up[:, 1])


def unpairs(tile0, tile1):
    joined = jnp.stack(swap(tile0, tile1), axis=1)
    return joined.reshape(2 * tile0.shape[0], *tile0.shape[1:])


def kernel(
    n, feat_hbm, taps_hbm, filt_hbm, skip_hbm, forward_hbm, backward_hbm, conv_in, queries_out, gated_out,
    feat, filt, taps_ref, skip_ref, forward, backward, fwd_high, fwd_low, bwd_high, bwd_low, rim_out, rim_in, queries, gated, sent_f, sent_g,
    got_f, got_g, f_re, f_im, f_sum, g_re, g_im, g_sum, conv_out,
    load_sem, store_sem, rim_send, rim_recv, send_sem, recv_sem,
):
    me = lax.axis_index("ctx")
    channels, tokens = filt.shape
    per = channels // n
    chunks = 2

    barrier = pltpu.get_barrier_semaphore()

    def greet(step, carry):
        pl.semaphore_signal(barrier, inc=1, device_id={"ctx": lax.rem(me + step, n)}, device_id_type=MESH)
        return carry

    lax.fori_loop(1, n, greet, 0, unroll=True)

    loads = [
        pltpu.make_async_copy(src, dst, load_sem.at[i])
        for i, (src, dst) in enumerate(
            [(feat_hbm, feat), (taps_hbm, taps_ref), (skip_hbm, skip_ref), (filt_hbm, filt), (forward_hbm, forward), (backward_hbm, backward)]
        )
    ]
    for load in loads:
        load.start()
    for load in loads[:3]:
        load.wait()
    scalars = jnp.concatenate(
        [taps_ref[0], taps_ref[1], taps_ref[2], skip_ref[...], jnp.zeros((TILE - 10, channels), jnp.float32)], axis=0
    )
    columns = jnp.transpose(scalars)

    def column(i):
        return jnp.broadcast_to(columns[:, i : i + 1], (channels, TILE))

    lane = lax.broadcasted_iota(jnp.int32, (channels, TILE), 1)
    ends = [feat[s, :, tokens - TILE :] for s in range(3)]
    merged = jnp.where(
        lane >= TILE - 2,
        ends[2],
        jnp.where(lane >= TILE - 4, pltpu.roll(ends[1], TILE - 2, 1), pltpu.roll(ends[0], TILE - 4, 1)),
    )
    rim_out[...] = jnp.transpose(merged)[TILE - 8 :, :]

    def pack(tile0, tile1, target):
        target[0], target[1] = swap(tile0.reshape(n, per, TILE), tile1.reshape(n, per, TILE))

    loads[3].wait()
    pack(filt[:, :TILE], filt[:, TILE:], sent_f)

    pl.semaphore_wait(barrier, n - 1)

    rim = pltpu.make_async_remote_copy(
        src_ref=rim_out, dst_ref=rim_in, send_sem=rim_send, recv_sem=rim_recv,
        device_id={"ctx": lax.rem(me + 1, n)}, device_id_type=MESH,
    )
    rim.start()

    def scatter(source, target, which, chunk):
        def send(step, carry):
            t = lax.rem(me + step, n)
            pltpu.make_async_remote_copy(
                src_ref=source.at[chunk, t], dst_ref=target.at[chunk, me], send_sem=send_sem.at[which, chunk], recv_sem=recv_sem.at[which, chunk],
                device_id={"ctx": t}, device_id_type=MESH,
            ).start()
            return carry

        lax.fori_loop(1, n, send, 0, unroll=True)
        pltpu.make_async_copy(source.at[chunk, me], target.at[chunk, me], recv_sem.at[which, chunk]).start()

    def wait_all(target, which, chunk):
        pltpu.make_async_copy(target.at[chunk], target.at[chunk], recv_sem.at[which, chunk]).wait()

    scatter(sent_f, got_f, 0, 0)
    for load in loads[4:]:
        load.wait()
    fwd_high[...], fwd_low[...] = split(forward[...])
    bwd_high[...], bwd_low[...] = split(backward[...])

    rim.wait()
    rims = jnp.transpose(jnp.concatenate([jnp.zeros((TILE - 8, channels), jnp.float32), rim_in[...]], axis=0))
    rims = jnp.where(me == 0, jnp.zeros_like(rims), rims)

    def featured(s):
        before = [pltpu.roll(rims, 2 * (2 - s) + lag, 1) for lag in (1, 2)]
        taps = [column(3 * s + j) for j in range(3)]
        parts = []
        for tile in range(tokens // TILE):
            own = feat[s, :, tile * TILE : (tile + 1) * TILE]
            total = taps[0] * own
            turned = []
            for lag in (1, 2):
                now = pltpu.roll(own, lag, 1)
                total = total + taps[lag] * jnp.where(lane < lag, before[lag - 1], now)
                turned.append(now)
            before = turned
            parts.append(total)
        return parts

    keys, values = featured(1), featured(2)
    products = [k * v for k, v in zip(keys, values)]
    pack(*products, sent_g)
    scatter(sent_g, got_g, 1, 0)
    scatter(sent_f, got_f, 0, 1)
    scatter(sent_g, got_g, 1, 1)
    skip = column(9)
    for tile, part in enumerate(featured(0)):
        at = slice(tile * TILE, (tile + 1) * TILE)
        queries[:, at] = part
        gated[:, at] = skip * products[tile]
    stores = [
        pltpu.make_async_copy(src, dst, store_sem.at[i]) for i, (src, dst) in enumerate([(queries, queries_out), (gated, gated_out)])
    ]
    for store in stores:
        store.start()

    def spectrum(blocks):
        rows = jnp.concatenate(pairs(blocks), axis=2).reshape(n * per // 2, tokens)
        bins = dot3(rows, fwd_high, fwd_low)
        tiles = [bins[:, i * TILE : (i + 1) * TILE].reshape(n // 2, per, TILE) for i in range(4)]
        return unpairs(tiles[0], tiles[1]), unpairs(tiles[2], tiles[3])

    turned = lax.axis_index("chan") // (lax.axis_size("chan") // 2)

    def turn(i, blocks):
        row = blocks // 2
        return row * (turned + (1 - 2 * turned) * (i // row)) + lax.rem(i, row)

    sign = (1 - 2 * (lax.broadcasted_iota(jnp.int32, (1, 1, TILE), 2) % 2)).astype(jnp.float32)
    nothing = jnp.zeros((PAD, per, TILE), jnp.float32)
    stage_blocks = n // 2

    def filter_spectra(chunk):
        wait_all(got_f, 0, chunk)
        real, imag = spectrum(got_f[chunk])
        f_re[...], f_im[...], f_sum[...] = real, imag, real + imag

    def signal_spectra(chunk):
        wait_all(got_g, 1, chunk)
        sums = []
        for part, store in zip(spectrum(got_g[chunk]), (g_re, g_im)):
            late = jnp.concatenate([nothing[:1], part[:-1]], axis=0)
            total = part + sign * late
            store[:PAD] = nothing
            store[PAD:] = total
            sums.append(total)
        g_sum[:PAD] = nothing
        g_sum[PAD:] = sums[0] + sums[1]

    def convolve(chunk):
        row = stage_blocks // 2
        for stage, blocks in ([(0, row), (1, row), (2, stage_blocks)] if chunk == chunks - 1 else [(0, stage_blocks), (2, stage_blocks)]):
            start = stage_blocks * lax.rem(me // stage_blocks + 1 + stage // 2, 2)
            if blocks == row:
                start = start + row * lax.rem(turned + stage, 2)
            pieces = []
            for first in range(0, blocks, GROUP):
                base = start + first

                def step(m, acc, base=base):
                    acc = list(acc)
                    fs = [[ref[GROUP * m + b] for ref in (f_re, f_im, f_sum)] for b in range(GROUP)]
                    g0 = base - GROUP * m + PAD
                    gs = {d: [ref[g0 + d] for ref in (g_re, g_im, g_sum)] for d in range(1 - GROUP, GROUP)}
                    for a in range(GROUP):
                        for b in range(GROUP):
                            for part in range(3):
                                acc[3 * a + part] = acc[3 * a + part] + fs[b][part] * gs[a - b][part]
                    return tuple(acc)

                zero = jnp.zeros((per, TILE), jnp.float32)
                acc = lax.fori_loop(0, base // GROUP + 1, step, (zero,) * (3 * GROUP))
                pieces += [acc[3 * a : 3 * a + 3] for a in range(GROUP)]
            both, cross, total = (jnp.stack([piece[part] for piece in pieces], axis=0) for part in range(3))
            real, imag = both - cross, total - both - cross
            packed = (lax.broadcasted_iota(jnp.int32, real.shape, 2) == 0) & (lax.broadcasted_iota(jnp.int32, real.shape, 1) < per // 2)
            real, imag = jnp.where(packed, both, real), jnp.where(packed, cross, imag)
            rows = jnp.concatenate([*pairs(real), *pairs(imag)], axis=2).reshape(blocks * per // 2, 2 * tokens)
            back = dot3(rows, bwd_high, bwd_low)
            tiles = [back[:, i * TILE : (i + 1) * TILE].reshape(blocks // 2, per, TILE) for i in range(2)]
            conv_out[chunk, pl.ds(start, blocks)] = unpairs(*tiles)

            def send(i, carry, start=start, blocks=blocks):
                if chunk < chunks - 1:
                    t = start + lax.rem(me + i, blocks)
                else:
                    t = start + (i if blocks == row else turn(i, blocks))

                @pl.when(t != me)
                def _():
                    pltpu.make_async_remote_copy(
                        src_ref=conv_out.at[chunk, t], dst_ref=conv_in.at[chunk, me], send_sem=send_sem.at[2, chunk], recv_sem=recv_sem.at[2, chunk],
                        device_id={"ctx": t}, device_id_type=MESH,
                    ).start()

                return carry

            lax.fori_loop(0, blocks, send, 0, unroll=True)
        pltpu.make_async_copy(conv_out.at[chunk, me], conv_in.at[chunk, me], recv_sem.at[2, chunk]).start()

    for chunk in range(chunks):
        filter_spectra(chunk)
        signal_spectra(chunk)
        convolve(chunk)

    for chunk in range(chunks):
        wait_all(conv_in, 2, chunk)
    for which in range(3):
        for chunk in range(chunks):
            sent = got_f.at[chunk, pl.ds(0, n - 1)]
            pltpu.make_async_copy(sent, sent, send_sem.at[which, chunk]).wait()
    for store in stores:
        store.wait()


def finish(conv_hbm, queries_hbm, gated_hbm, out_hbm, conv, queries, gated, out, load_sem, store_sem):
    parts = load_sem.shape[1]
    n, per = conv.shape[1:3]
    loads, stores = [], []
    for i in range(parts):
        blocks, rows = pl.ds(i * n // parts, n // parts), pl.ds(i * n * per // parts, n * per // parts)
        views = [(conv_hbm.at[:, blocks], conv.at[:, blocks]), (queries_hbm.at[rows], queries.at[rows]), (gated_hbm.at[rows], gated.at[rows])]
        loads.append([pltpu.make_async_copy(src, dst, load_sem.at[j, i]) for j, (src, dst) in enumerate(views)])
        stores.append(pltpu.make_async_copy(out.at[rows], out_hbm.at[rows], store_sem.at[i]))
        for load in loads[-1]:
            load.start()
    for i in range(parts):
        blocks, rows = pl.ds(i * n // parts, n // parts), pl.ds(i * n * per // parts, n * per // parts)
        for load in loads[i]:
            load.wait()
        for tile, part in enumerate(swap(conv[0, blocks], conv[1, blocks])):
            at = slice(tile * TILE, (tile + 1) * TILE)
            out[rows, at] = queries[rows, at] * (part.reshape(n * per // parts, TILE) + gated[rows, at])
        stores[i].start()
    for store in stores:
        store.wait()


def solution(mesh):
    n = mesh.shape["ctx"]

    def shards(features, short_conv, filters, skip_gain):
        channels, tokens = filters.shape
        per = channels // n
        any_space = pl.BlockSpec(memory_space=pl.ANY)
        real = functools.partial(pltpu.VMEM, dtype=jnp.float32)
        moved, spectra, padded = (2, n, per, TILE), (n, per, TILE), (n + PAD, per, TILE)
        whole = jax.ShapeDtypeStruct((channels, tokens), jnp.float32)
        arrived = pl.pallas_call(
            functools.partial(kernel, n),
            out_shape=(jax.ShapeDtypeStruct(moved, jnp.float32), whole, whole),
            in_specs=[any_space] * 6,
            out_specs=(any_space,) * 3,
            scratch_shapes=[
                real((3, channels, tokens)),
                real((channels, tokens)),
                real((3, 3, channels)),
                real((1, channels)),
                real((tokens, 2 * tokens)),
                real((2 * tokens, tokens)),
                pltpu.VMEM((tokens, 2 * tokens), jnp.bfloat16),
                pltpu.VMEM((tokens, 2 * tokens), jnp.bfloat16),
                pltpu.VMEM((2 * tokens, tokens), jnp.bfloat16),
                pltpu.VMEM((2 * tokens, tokens), jnp.bfloat16),
                real((8, channels)),
                real((8, channels)),
                real((channels, tokens)),
                real((channels, tokens)),
                real(moved),
                real(moved),
                real(moved),
                real(moved),
                real(spectra),
                real(spectra),
                real(spectra),
                real(padded),
                real(padded),
                real(padded),
                real(moved),
                pltpu.SemaphoreType.DMA((6,)),
                pltpu.SemaphoreType.DMA((2,)),
                pltpu.SemaphoreType.DMA,
                pltpu.SemaphoreType.DMA,
                pltpu.SemaphoreType.DMA((3, 2)),
                pltpu.SemaphoreType.DMA((3, 2)),
            ],
            compiler_params=pltpu.CompilerParams(collective_id=0, has_side_effects=True, vmem_limit_bytes=LIMIT),
        )(features, jnp.transpose(short_conv, (0, 2, 1)), filters, skip_gain.reshape(1, channels), *(jnp.asarray(t) for t in tables(tokens)))
        parts = 1
        return pl.pallas_call(
            finish,
            out_shape=whole,
            in_specs=[any_space] * 3,
            out_specs=any_space,
            scratch_shapes=[
                real(moved),
                real((channels, tokens)),
                real((channels, tokens)),
                real((channels, tokens)),
                pltpu.SemaphoreType.DMA((3, parts)),
                pltpu.SemaphoreType.DMA((parts,)),
            ],
            compiler_params=pltpu.CompilerParams(vmem_limit_bytes=LIMIT),
        )(*arrived)

    placed = (P(None, "chan", "ctx"), P(None, "chan", None), P("chan", "ctx"), P("chan"))
    return jax.shard_map(shards, mesh=mesh, in_specs=placed, out_specs=P("chan", "ctx"), check_vma=False)
```
